256 devices in a mesh: wide: 64 (over z, x, core), narrow: 4 (over y).
Axes of the slice: x: 4, y: 4, z: 8, core: 2. Of those that a mesh axis runs over, the one named last changes fastest.
Arguments:
- embeddings: bfloat16 [524288, 1536], P(('wide', 'narrow')), may hold values from -400 to 400
- test_matrix: bfloat16 [1536, 256], replicated, may hold values from -0.15625 to 0.15625
Outputs:
- basis: float32 [524288, 256], P(('wide', 'narrow'))
- loadings: float32 [1536, 256], P('wide')
The draws below stay inside these ranges and needn't reach their ends.
All inputs are finite; a program needn't handle non-finite values.
Results may differ from the reference program's by a relative error of at most 0.0043.
Values sent between devices are 32-bit elements; how exact they have to be, the bound alone decides.
No kernel may reach another device: no remote copies, remote signals or barrier semaphores. Data moves between devices by JAX's collectives and lax.ppermute only.
A program may use at most 64 MiB of HBM per device.

```python
import math
import jax
import jax.numpy as jnp
from jax import lax

F = 1536
K = 256
ROWS = 524288
GROUP_ROWS = 8192
COLS_DEV = 24


def draw_embeddings(key, part):
    key = jax.random.fold_in(key, 11)
    key_noise, key_rows, key_cols, key_pair = jax.random.split(key, 4)
    row_index = jnp.arange(ROWS, dtype=jnp.int32)
    position = row_index.astype(jnp.float32) / ROWS
    row_level = jax.random.uniform(key_rows, (ROWS,), jnp.float32)
    col_level = jax.random.uniform(key_cols, (F,), jnp.float32)
    pairing = jax.random.permutation(key_pair, F // COLS_DEV)
    row_group = row_index // GROUP_ROWS
    column_group = jnp.arange(F, dtype=jnp.int32) // COLS_DEV
    spiked = jnp.where(pairing[row_group][:, None] == column_group[None, :], 3.0, 1.0)
    rise = math.log(3.0)
    noise = jnp.clip(jax.random.normal(key_noise, (ROWS, F), jnp.float32), -5.0, 5.0)
    row_scale = jnp.exp(row_level * math.log(10.0) + rise * position)
    col_scale = jnp.exp(col_level * math.log(10.0))
    values = noise * row_scale[:, None] * col_scale[None, :] * spiked / 40.0
    return values.astype(jnp.bfloat16)


def normal_values(stream_key, shape, deviation, bound, held_as=jnp.bfloat16):
    result = deviation * jax.random.normal(stream_key, shape, jnp.float32)
    return jnp.clip(result, min=-bound, max=bound).astype(held_as)


def setup_inputs(seed: int = 0) -> dict:
    arg_keys = jax.random.split(jax.random.key(seed), 3)
    return {
        "embeddings": draw_embeddings(jax.random.fold_in(arg_keys[2], 71), 0),
        "test_matrix": normal_values(arg_keys[1], (F, K), F ** -0.5, 0.15625),
    }


def factor_inverse(gram):
    order = gram.shape[0]
    lower = jnp.linalg.cholesky(gram)
    identity = jnp.eye(order, dtype=gram.dtype)
    return jax.scipy.linalg.solve_triangular(lower, identity, trans='T', lower=True)

def reference(embeddings, test_matrix):
    sketch = jnp.dot(embeddings.astype(jnp.float32), test_matrix.astype(jnp.float32), preferred_element_type=jnp.float32).astype(jnp.bfloat16)
    gram_mean = jnp.dot(sketch.T.astype(jnp.float32), sketch.astype(jnp.float32), preferred_element_type=jnp.float32) / ROWS
    inverse = factor_inverse(gram_mean)
    basis = jnp.dot(sketch.astype(jnp.float32), inverse, precision=lax.Precision.HIGHEST)
    cross = jnp.dot(embeddings.T.astype(jnp.float32), sketch.astype(jnp.float32), preferred_element_type=jnp.float32)
    loadings = jnp.dot(cross, inverse, precision=lax.Precision.HIGHEST) / ROWS
    return (basis, loadings)
```

```python
import functools

import jax
import jax.numpy as jnp
from jax import lax
from jax.experimental import pallas as pl
from jax.experimental.pallas import tpu as pltpu
from jax.sharding import PartitionSpec as P

LANES = 128
SUB = 8
CHUNK = 256


def barrier(*values):
    return lax.optimization_barrier(values)


def shifted(x, axis, target):
    return lax.ppermute(x, axis, [(i, target(i)) for i in range(lax.axis_size(axis))])


def along_z(target):
    return lambda i: (target(i >> 3) % 8) << 3 | i & 7


Z_PAIR = along_z(lambda z: z ^ 1)
Z_NEXT = along_z(lambda z: z + 1 if z % 2 else z - 1)
Z_TWO = along_z(lambda z: z + 2 if z % 2 else z - 2)
Z_THREE = along_z(lambda z: z + 3 if z % 2 else z - 3)


def along_x(bits):
    return lambda i: i ^ bits << 1


def other_core(i):
    return i ^ 1


def flip(bits):
    return lambda i: i ^ bits


def sum4(parts):
    return (parts[0] + parts[1]) + (parts[2] + parts[3])


def splat(x, sub=None, lane=None):
    if lane is not None:
        x = x[:, lane : lane + 1]
    if sub is not None:
        x = x[sub : sub + 1, :]
    return jnp.broadcast_to(x, (SUB, LANES))


def factor_in_place(s, order):
    halves = order // LANES
    row = lax.broadcasted_iota(jnp.int32, (SUB, LANES), 0)
    lane = lax.broadcasted_iota(jnp.int32, (SUB, LANES), 1)

    def tile(r, h):
        return (slice(r, r + SUB), slice(LANES * h, LANES * (h + 1)))

    for p0 in range(0, order, LANES):
        p1 = p0 + LANES
        here = p0 // LANES
        for r0 in range(p0, p1, SUB):
            l0 = r0 - p0
            last = r0 + SUB >= p1
            fwd = [s[tile(r0, h)] for h in range(halves)]
            cols = [splat(fwd[here], lane=l0 + k) for k in range(SUB)]
            pivots = (lane >= l0) & (lane < l0 + SUB)
            fwd[here] = jnp.where(pivots, jnp.where(lane - l0 == row, 1.0, 0.0), fwd[here])
            both = list(fwd)
            inv_d = jnp.zeros((SUB, LANES), jnp.float32)
            for i in range(SUB):
                recip = 1.0 / splat(cols[i], sub=i)
                mult = cols[i] * recip
                below = jnp.where(row > i, mult, 0.0)
                others = jnp.where(row != i, mult, 0.0)
                inv_d = jnp.where(row == i, recip, inv_d)
                for k in range(i + 1, SUB):
                    cols[k] = cols[k] - (below if last else others) * splat(cols[k], sub=i)
                for h in range(halves):
                    pivot_row = splat(fwd[h], sub=i)
                    fwd[h] = fwd[h] - below * pivot_row
                    if not last:
                        both[h] = both[h] - others * pivot_row
            if not last:
                both = [b * inv_d for b in both]
                rows = [[splat(b, sub=k) for b in both] for k in range(SUB)]
                for g0 in range(r0 + SUB, p1, SUB):
                    old = [s[tile(g0, h)] for h in range(halves)]
                    coef = [splat(old[here], lane=l0 + k) for k in range(SUB)]
                    old[here] = jnp.where(pivots, 0.0, old[here])
                    for h in range(halves):
                        t = [coef[k] * rows[k][h] for k in range(SUB)]
                        s[tile(g0, h)] = old[h] - (sum4(t[:4]) + sum4(t[4:]))
            scale = jnp.sqrt(inv_d)
            for h in range(halves):
                s[tile(r0, h)] = fwd[h] * scale
        if p1 < order:
            panel = s[p0:p1, :]
            r = lax.broadcasted_iota(jnp.int32, panel.shape, 0)
            c = lax.broadcasted_iota(jnp.int32, panel.shape, 1)
            panel = jnp.where((c < p1) & (c > p0 + r), 0.0, panel)
            update = lax.dot_general(
                panel[:, p1:],
                panel,
                (((0,), (0,)), ((), ())),
                precision=lax.Precision.HIGHEST,
                preferred_element_type=jnp.float32,
            )
            c = lax.broadcasted_iota(jnp.int32, update.shape, 1)
            s[p1:, :] = jnp.where((c >= p0) & (c < p1), 0.0, s[p1:, :]) - update


def basis_kernel(core, mine, other, sketch, inv_t, basis, s, out, sems):
    first = core[0] == 0
    half = mine.shape[0]
    a, b = mine[...], other[...]
    low = jnp.where(first, a, b)
    high = jnp.where(first, b, a)
    s[:LANES, :LANES] = low[:LANES]
    s[: half - LANES, LANES:] = low[LANES:]
    s[half - LANES : LANES, LANES:] = high[: 2 * LANES - half]
    s[LANES:, LANES:] = high[2 * LANES - half :]
    order = s.shape[0]
    factor_in_place(s, order)
    r = lax.broadcasted_iota(jnp.int32, s.shape, 0)
    c = lax.broadcasted_iota(jnp.int32, s.shape, 1)
    inv = jnp.where(c <= r, s[...], 0.0)
    inv_t[...] = inv
    hi = inv.astype(jnp.bfloat16)
    rest = inv - hi.astype(jnp.float32)
    mid = rest.astype(jnp.bfloat16)
    low = (rest - mid.astype(jnp.float32)).astype(jnp.bfloat16)
    copies = []
    for n in range(sketch.shape[0] // CHUNK):
        rows = slice(n * CHUNK, (n + 1) * CHUNK)
        x = sketch[rows, :]
        total = None
        for part in (low, mid, hi):
            term = lax.dot_general(
                x, part, (((1,), (1,)), ((), ())), preferred_element_type=jnp.float32
            )
            total = term if total is None else total + term
        out[rows, :] = total
        copy = pltpu.make_async_copy(out.at[rows, :], basis.at[rows, :], sems.at[n])
        copy.start()
        copies.append(copy)
    for copy in copies:
        copy.wait()


def finish(core, mine, other, sketch):
    rows, order = sketch.shape
    vmem = pl.BlockSpec(memory_space=pltpu.VMEM)
    return pl.pallas_call(
        basis_kernel,
        out_shape=(
            jax.ShapeDtypeStruct((order, order), jnp.float32),
            jax.ShapeDtypeStruct((rows, order), jnp.float32),
        ),
        in_specs=[pl.BlockSpec(memory_space=pltpu.SMEM), vmem, vmem, vmem],
        out_specs=(vmem, pl.BlockSpec(memory_space=pl.ANY)),
        scratch_shapes=[
            pltpu.VMEM((order, order), jnp.float32),
            pltpu.VMEM((rows, order), jnp.float32),
            pltpu.SemaphoreType.DMA((rows // CHUNK,)),
        ],
        compiler_params=pltpu.CompilerParams(vmem_limit_bytes=24 * 2**20),
    )(core, mine, other, sketch)


def pick(x, index):
    return lax.dynamic_index_in_dim(x, index, 0, keepdims=False)


def body(embeddings, test_matrix):
    n_wide = lax.axis_size("wide")
    rows_total = embeddings.shape[0] * n_wide * lax.axis_size("narrow")
    place = lax.axis_index("wide")
    core, x_at, z_at = place & 1, place >> 1 & 3, place >> 3
    sketch = jnp.dot(embeddings, test_matrix, preferred_element_type=jnp.float32).astype(
        jnp.bfloat16
    )
    gram = (
        lax.dot_general(
            sketch, sketch, (((0,), (0,)), ((), ())), preferred_element_type=jnp.float32
        )
        / rows_total
    )
    packed = jnp.concatenate([gram[:LANES, :LANES], gram[:LANES, LANES:], gram[LANES:, LANES:]])
    top, bottom = jnp.split(packed, 2)
    mine = jnp.where(core == 0, top, bottom)
    theirs = jnp.where(core == 0, bottom, top)
    mine = mine + shifted(theirs, "wide", other_core)

    cross = lax.dot_general(
        embeddings, sketch, (((0,), (0,)), ((), ())), preferred_element_type=jnp.float32
    )
    owned = cross.shape[0] // n_wide
    cross = cross.reshape(8, 4, 2, owned, cross.shape[1])
    kept = jnp.where(core == 0, cross[:, :, 0], cross[:, :, 1])
    given = jnp.where(core == 0, cross[:, :, 1], cross[:, :, 0])
    mine, kept, given = barrier(mine, kept, given)

    mine = mine + shifted(mine, "wide", Z_PAIR)
    kept = (kept + shifted(given, "wide", other_core)).transpose(1, 0, 2, 3)
    mine, kept = barrier(mine, kept)

    if CROSS == "a2a":
        groups_x = [[z * 8 + x * 2 + c for x in range(4)] for z in range(8) for c in range(2)]
        groups_z = [[z * 8 + r for z in range(8)] for r in range(8)]
        kx = lax.all_to_all(kept, "wide", 0, 0, tiled=True, axis_index_groups=groups_x)
        mine = sum4([mine] + [shifted(mine, "wide", t) for t in (Z_NEXT, Z_TWO, Z_THREE)])
        mine, = barrier(mine)
        mine = sum4([mine] + [shifted(mine, "narrow", flip(k)) for k in (1, 2, 3)])
        mine, kept = barrier(mine, kx)
        kept = jnp.sum(kept, axis=0)
        kz = lax.all_to_all(kept, "wide", 0, 0, tiled=True, axis_index_groups=groups_z)
        mine = sum4([mine] + [shifted(mine, "wide", along_x(k)) for k in (1, 2, 3)])
        mine, = barrier(mine)
        other = shifted(mine, "wide", other_core)
        other, kept = barrier(other, kz)
        kept = jnp.sum(kept, axis=0)
    else:
        parts = [pick(kept, x_at ^ k) for k in range(4)]
        mine = sum4([mine] + [shifted(mine, "wide", t) for t in (Z_NEXT, Z_TWO, Z_THREE)])
        kept = sum4(parts[:1] + [shifted(parts[k], "wide", along_x(k)) for k in (1, 2, 3)])
        mine, kept = barrier(mine, kept)
        kept = kept.reshape(4, 2, owned, -1)
        parts = [pick(kept, (z_at >> 1) ^ k) for k in range(4)]
        mine = sum4([mine] + [shifted(mine, "narrow", flip(k)) for k in (1, 2, 3)])
        kept = sum4(
            parts[:1]
            + [shifted(parts[k], "wide", along_z(lambda z, k=k: z ^ 2 * k)) for k in (1, 2, 3)]
        )
        mine, kept = barrier(mine, kept)
        parts = [pick(kept, (z_at & 1) ^ k) for k in range(2)]
        mine = sum4([mine] + [shifted(mine, "wide", along_x(k)) for k in (1, 2, 3)])
        kept = parts[0] + shifted(parts[1], "wide", Z_PAIR)
        mine, kept = barrier(mine, kept)
        other = shifted(mine, "wide", other_core)
    kept = sum4([kept] + [shifted(kept, "narrow", flip(k)) for k in (1, 2, 3)])
    inv_t, basis_rows = finish(core.reshape(1), mine, other, sketch)
    loadings = (
        lax.dot_general(
            kept, inv_t, (((1,), (1,)), ((), ())), precision=lax.Precision.HIGHEST
        )
        / rows_total
    )
    return (basis_rows, loadings)


CROSS = "a2a"


def solution(mesh):
    in_specs = (P(("wide", "narrow"), None), P())
    out_specs = (P(("wide", "narrow"), None), P("wide", None))
    return jax.shard_map(body, mesh=mesh, in_specs=in_specs, out_specs=out_specs, check_vma=False)
```

```python
import functools

import jax
import jax.numpy as jnp
from jax import lax
from jax.experimental import pallas as pl
from jax.experimental.pallas import tpu as pltpu
from jax.sharding import PartitionSpec as P

LANES = 128
SUB = 8
PANEL = 64
CHUNK = 256
LOAD = 512
AHEAD = 2


def barrier(*values):
    return lax.optimization_barrier(values)


def shifted(x, axis, target):
    return lax.ppermute(x, axis, [(i, target(i)) for i in range(lax.axis_size(axis))])


def along_z(target):
    return lambda i: (target(i >> 3) % 8) << 3 | i & 7


Z_PAIR = along_z(lambda z: z ^ 1)
Z_NEXT = along_z(lambda z: z + 1 if z % 2 else z - 1)
Z_TWO = along_z(lambda z: z + 2 if z % 2 else z - 2)
Z_THREE = along_z(lambda z: z + 3 if z % 2 else z - 3)


def along_x(bits):
    return lambda i: i ^ bits << 1


def other_core(i):
    return i ^ 1


def flip(bits):
    return lambda i: i ^ bits


def sum4(parts):
    return (parts[0] + parts[1]) + (parts[2] + parts[3])


def over_four(x, axis, flipped):
    one, three, two = (shifted(x, axis, flipped(k)) for k in (1, 3, 2))
    return sum4([x, one, two, three])


def splat(x, sub=None, lane=None):
    if lane is not None:
        x = x[:, lane : lane + 1]
    if sub is not None:
        x = x[sub : sub + 1, :]
    return jnp.broadcast_to(x, (SUB, LANES))


def sum8(parts):
    return sum4(parts[:4]) + sum4(parts[4:])


def factor_in_place(s, order):
    halves = order // LANES
    row = lax.broadcasted_iota(jnp.int32, (SUB, LANES), 0)
    lane = lax.broadcasted_iota(jnp.int32, (SUB, LANES), 1)

    def tile(r, h):
        return (slice(r, r + SUB), slice(LANES * h, LANES * (h + 1)))

    for p0 in range(0, order, PANEL):
        p1, here = p0 + PANEL, p0 // LANES
        cols = [splat(s[tile(p0, here)], lane=p0 % LANES + k) for k in range(SUB)]
        for r0 in range(p0, p1, SUB):
            l0 = r0 % LANES
            last = r0 + SUB >= p1
            fwd = [s[tile(r0, h)] for h in range(halves)]
            if not last:
                ahead = [splat(fwd[here], lane=l0 + SUB + k) for k in range(SUB)]
                below = s[tile(r0 + SUB, here)]
                next_coef = [splat(below, lane=l0 + k) for k in range(SUB)]
                next_cols = [splat(below, lane=l0 + SUB + k) for k in range(SUB)]
            pivots = (lane >= l0) & (lane < l0 + SUB)
            fwd[here] = jnp.where(pivots, jnp.where(lane - l0 == row, 1.0, 0.0), fwd[here])
            both = list(fwd)
            inv_d = jnp.zeros((SUB, LANES), jnp.float32)
            for i in range(0, SUB, 2):
                j = i + 1
                a, b, c = splat(cols[i], sub=i), splat(cols[i], sub=j), splat(cols[j], sub=j)
                inv_det, inv_a = 1.0 / (a * c - b * b), 1.0 / a
                pair = (row == i) | (row == j)
                ci = jnp.where(row == i, -1.0, jnp.where(row == j, 0.0, cols[i]))
                cj = jnp.where(row == j, -1.0, jnp.where(row == i, 0.0, cols[j]))
                mi = (ci * c - cj * b) * inv_det
                mj = (cj * a - ci * b) * inv_det
                fi = jnp.where(row > j, mi, jnp.where(row == j, b * inv_a, 0.0))
                fj = jnp.where(row > j, mj, 0.0)
                inv_d = jnp.where(row == i, inv_a, jnp.where(row == j, a * inv_det, inv_d))

                def eliminated(x):
                    x_i, x_j = splat(x, sub=i), splat(x, sub=j)
                    return jnp.where(pair, 0.0, x) - (mi * x_i + mj * x_j)

                for k in range(j + 1, SUB):
                    cols[k] = eliminated(cols[k])
                fwd = [x - (fi * splat(x, sub=i) + fj * splat(x, sub=j)) for x in fwd]
                if not last:
                    ahead = [eliminated(x) for x in ahead]
                    both = [eliminated(x) for x in both]
            if not last:
                cols = [
                    next_cols[k] - sum8([next_coef[m] * splat(ahead[k], sub=m) for m in range(SUB)])
                    for k in range(SUB)
                ]
                rows = [[splat(x, sub=k) for x in both] for k in range(SUB)]
                for g0 in range(r0 + SUB, p1, SUB):
                    old = [s[tile(g0, h)] for h in range(halves)]
                    coef = next_coef
                    if g0 > r0 + SUB:
                        coef = [splat(old[here], lane=l0 + k) for k in range(SUB)]
                    old[here] = jnp.where(pivots, 0.0, old[here])
                    for h in range(halves):
                        change = sum8([coef[k] * rows[k][h] for k in range(SUB)])
                        s[tile(g0, h)] = old[h] - change
            scale = jnp.sqrt(inv_d)
            for h in range(halves):
                s[tile(r0, h)] = fwd[h] * scale
        if p1 < order:
            panel = s[p0:p1, :]
            r = lax.broadcasted_iota(jnp.int32, panel.shape, 0)
            c = lax.broadcasted_iota(jnp.int32, panel.shape, 1)
            panel = jnp.where((c < p1) & (c > p0 + r), 0.0, panel)
            update = lax.dot_general(
                panel[:, p1:],
                panel,
                (((0,), (0,)), ((), ())),
                precision=lax.Precision.HIGHEST,
                preferred_element_type=jnp.float32,
            )
            c = lax.broadcasted_iota(jnp.int32, update.shape, 1)
            s[p1:, :] = jnp.where((c >= p0) & (c < p1), 0.0, s[p1:, :]) - update


def factor_kernel(core, mine, other, inv_t, s):
    first = core[0] == 0
    half = mine.shape[0]
    a, b = mine[...], other[...]
    low = jnp.where(first, a, b)
    high = jnp.where(first, b, a)
    s[:LANES, :LANES] = low[:LANES]
    s[: half - LANES, LANES:] = low[LANES:]
    s[half - LANES : LANES, LANES:] = high[: 2 * LANES - half]
    s[LANES:, LANES:] = high[2 * LANES - half :]
    factor_in_place(s, s.shape[0])
    r = lax.broadcasted_iota(jnp.int32, s.shape, 0)
    c = lax.broadcasted_iota(jnp.int32, s.shape, 1)
    inv_t[...] = jnp.where(c <= r, s[...], 0.0)


def factor(core, mine, other):
    order = 2 * LANES
    vmem = pl.BlockSpec(memory_space=pltpu.VMEM)
    return pl.pallas_call(
        factor_kernel,
        out_shape=jax.ShapeDtypeStruct((order, order), jnp.float32),
        in_specs=[pl.BlockSpec(memory_space=pltpu.SMEM), vmem, vmem],
        out_specs=vmem,
        scratch_shapes=[pltpu.VMEM((order, order), jnp.float32)],
        compiler_params=pltpu.CompilerParams(vmem_limit_bytes=16 * 2**20),
        cost_estimate=pl.CostEstimate(flops=0, bytes_accessed=20 * 2**20, transcendentals=0),
    )(core, mine, other)


def basis_kernel(sketch, inv_t, basis, out, sems):
    inv = inv_t[...]
    hi = inv.astype(jnp.bfloat16)
    mid = (inv - hi.astype(jnp.float32)).astype(jnp.bfloat16)
    copies = []
    for n in range(sketch.shape[0] // CHUNK):
        rows = slice(n * CHUNK, (n + 1) * CHUNK)
        x = sketch[rows, :]
        total = None
        for part in (mid, hi):
            term = lax.dot_general(
                x, part, (((1,), (1,)), ((), ())), preferred_element_type=jnp.float32
            )
            total = term if total is None else total + term
        out[rows, :] = total
        copies.append(pltpu.make_async_copy(out.at[rows, :], basis.at[rows, :], sems.at[n]))
        copies[-1].start()
    for copy in copies:
        copy.wait()


def basis_of(sketch, inv_t):
    rows, order = sketch.shape
    vmem = pl.BlockSpec(memory_space=pltpu.VMEM)
    return pl.pallas_call(
        basis_kernel,
        out_shape=jax.ShapeDtypeStruct((rows, order), jnp.float32),
        in_specs=[vmem, vmem],
        out_specs=pl.BlockSpec(memory_space=pl.ANY),
        scratch_shapes=[
            pltpu.VMEM((rows, order), jnp.float32),
            pltpu.SemaphoreType.DMA((rows // CHUNK,)),
        ],
        compiler_params=pltpu.CompilerParams(vmem_limit_bytes=16 * 2**20),
        cost_estimate=pl.CostEstimate(
            flops=4 * rows * order * order, bytes_accessed=6 * rows * order, transcendentals=0
        ),
    )(sketch, inv_t)


def front_kernel(core, e, t, sketch, mine, theirs, kept, given, e_kept, t_kept, sems, *, scale):
    steps = e.shape[0] // LOAD
    load_t = pltpu.make_async_copy(t, t_kept, sems.at[steps])
    load_t.start()
    blocks = [slice(n * LOAD, (n + 1) * LOAD) for n in range(steps)]
    loads = [
        pltpu.make_async_copy(e.at[rows, :], e_kept.at[rows, :], sems.at[n])
        for n, rows in enumerate(blocks)
    ]
    for load in loads[:AHEAD]:
        load.start()
    load_t.wait()
    for n, rows in enumerate(blocks):
        loads[n].wait()
        if n + AHEAD < steps:
            loads[n + AHEAD].start()
        sketch[rows, :] = jnp.dot(
            e_kept[rows, :], t_kept[...], preferred_element_type=jnp.float32
        ).astype(jnp.bfloat16)
    s = sketch[...]
    by_rows = (((0,), (0,)), ((), ()))
    gram = lax.dot_general(s, s, by_rows, preferred_element_type=jnp.float32)
    packed = [gram[:LANES, :LANES], gram[:LANES, LANES:], gram[LANES:, LANES:]]
    packed = jnp.concatenate(packed, axis=0) * scale
    half = packed.shape[0] // 2
    first = core[0] == 0
    mine[...] = jnp.where(first, packed[:half], packed[half:])
    theirs[...] = jnp.where(first, packed[half:], packed[:half])
    n_x, n_z, owned, order = kept.shape
    per_z = 2 * n_x * owned
    for z in range(0, n_z, 2):
        feats = slice(z * per_z, (z + 2) * per_z)
        c = lax.dot_general(
            e_kept[:, feats], s, by_rows, preferred_element_type=jnp.float32
        )
        c = c.reshape(2, n_x, 2, owned, order)
        for dz in range(2):
            for x in range(n_x):
                kept[x, z + dz] = jnp.where(first, c[dz, x, 0], c[dz, x, 1])
                given[x, z + dz] = jnp.where(first, c[dz, x, 1], c[dz, x, 0])


def front(core, e, t, rows_total, n_x, n_z):
    rows, feats = e.shape
    order = t.shape[1]
    gram_half = jax.ShapeDtypeStruct((3 * LANES // 2, LANES), jnp.float32)
    owned = feats // (2 * n_x * n_z)
    cross_half = jax.ShapeDtypeStruct((n_x, n_z, owned, order), jnp.float32)
    vmem = pl.BlockSpec(memory_space=pltpu.VMEM)
    hbm = pl.BlockSpec(memory_space=pltpu.HBM)
    return pl.pallas_call(
        functools.partial(front_kernel, scale=1.0 / rows_total),
        out_shape=(
            jax.ShapeDtypeStruct((rows, order), jnp.bfloat16),
            gram_half,
            gram_half,
            cross_half,
            cross_half,
        ),
        in_specs=[pl.BlockSpec(memory_space=pltpu.SMEM), hbm, hbm],
        out_specs=(vmem,) * 5,
        scratch_shapes=[
            pltpu.VMEM(e.shape, e.dtype),
            pltpu.VMEM(t.shape, t.dtype),
            pltpu.SemaphoreType.DMA((rows // LOAD + 1,)),
        ],
        compiler_params=pltpu.CompilerParams(vmem_limit_bytes=52 * 2**20),
    )(core, e, t)


def pick(x, index):
    return lax.dynamic_index_in_dim(x, index, 0, keepdims=False)


def body(embeddings, test_matrix):
    n_wide = lax.axis_size("wide")
    rows_total = embeddings.shape[0] * n_wide * lax.axis_size("narrow")
    place = lax.axis_index("wide")
    core, x_at, z_at = place & 1, place >> 1 & 3, place >> 3
    at = core.reshape(1)
    sketch, mine, theirs, kept, given = front(at, embeddings, test_matrix, rows_total, 4, 8)
    groups_x = [[z * 8 + x * 2 + c for x in range(4)] for z in range(8) for c in range(2)]
    groups_z = [[z * 8 + r for z in range(8)] for r in range(8)]
    mine = mine + shifted(theirs, "wide", other_core)
    kept = kept + shifted(given, "wide", other_core)
    kept = lax.all_to_all(kept, "wide", 0, 0, tiled=True, axis_index_groups=groups_x)
    mine = mine + shifted(mine, "wide", Z_PAIR)
    mine, = barrier(mine)
    mine = sum4([mine] + [shifted(mine, "wide", t) for t in (Z_NEXT, Z_TWO, Z_THREE)])
    kept = jnp.sum(kept, axis=0)
    kept = lax.all_to_all(kept, "wide", 0, 0, tiled=True, axis_index_groups=groups_z)
    mine, = barrier(mine)
    mine = over_four(mine, "narrow", flip)
    mine, = barrier(mine)
    mine = over_four(mine, "wide", along_x)
    mine, = barrier(mine)
    other = shifted(mine, "wide", other_core)
    inv_t = factor(at, mine, other)
    inv_t, kept = barrier(inv_t, kept)
    kept = jnp.sum(kept, axis=0)
    kept = over_four(kept, "narrow", flip)
    basis_rows = basis_of(sketch, inv_t)
    loadings = (
        lax.dot_general(
            kept, inv_t, (((1,), (1,)), ((), ())), precision=lax.Precision.HIGHEST
        )
        / rows_total
    )
    return (basis_rows, loadings)


CROSS = "a2a"


def solution(mesh):
    in_specs = (P(("wide", "narrow"), None), P())
    out_specs = (P(("wide", "narrow"), None), P("wide", None))
    return jax.shard_map(body, mesh=mesh, in_specs=in_specs, out_specs=out_specs, check_vma=False)
```

```python
import functools

import jax
import jax.numpy as jnp
from jax import lax
from jax.experimental import pallas as pl
from jax.experimental.pallas import tpu as pltpu
from jax.sharding import PartitionSpec as P

LANES = 128
SUB = 8
PANEL = 64
CHUNK = 256
LOAD = 512
AHEAD = 2


def barrier(*values):
    return lax.optimization_barrier(values)


def shifted(x, axis, target):
    return lax.ppermute(x, axis, [(i, target(i)) for i in range(lax.axis_size(axis))])


def along_z(target):
    return lambda i: (target(i >> 3) % 8) << 3 | i & 7


Z_PAIR = along_z(lambda z: z ^ 1)
Z_NEXT = along_z(lambda z: z + 1 if z % 2 else z - 1)
Z_TWO = along_z(lambda z: z + 2 if z % 2 else z - 2)
Z_THREE = along_z(lambda z: z + 3 if z % 2 else z - 3)


def along_x(bits):
    return lambda i: i ^ bits << 1


def other_core(i):
    return i ^ 1


def flip(bits):
    return lambda i: i ^ bits


def sum4(parts):
    return (parts[0] + parts[1]) + (parts[2] + parts[3])


def over_four(x, axis, flipped):
    one, three, two = (shifted(x, axis, flipped(k)) for k in (1, 3, 2))
    return sum4([x, one, two, three])


def splat(x, sub=None, lane=None):
    if lane is not None:
        x = x[:, lane : lane + 1]
    if sub is not None:
        x = x[sub : sub + 1, :]
    return jnp.broadcast_to(x, (SUB, LANES))


def sum8(parts):
    return sum4(parts[:4]) + sum4(parts[4:])


def factor_in_place(s, order):
    halves = order // LANES
    row = lax.broadcasted_iota(jnp.int32, (SUB, LANES), 0)
    lane = lax.broadcasted_iota(jnp.int32, (SUB, LANES), 1)

    def tile(r, h):
        return (slice(r, r + SUB), slice(LANES * h, LANES * (h + 1)))

    for p0 in range(0, order, PANEL):
        p1, here = p0 + PANEL, p0 // LANES
        cols = [splat(s[tile(p0, here)], lane=p0 % LANES + k) for k in range(SUB)]
        for r0 in range(p0, p1, SUB):
            l0 = r0 % LANES
            last = r0 + SUB >= p1
            fwd = [s[tile(r0, h)] for h in range(halves)]
            if not last:
                ahead = [splat(fwd[here], lane=l0 + SUB + k) for k in range(SUB)]
                below = s[tile(r0 + SUB, here)]
                next_coef = [splat(below, lane=l0 + k) for k in range(SUB)]
                next_cols = [splat(below, lane=l0 + SUB + k) for k in range(SUB)]
            pivots = (lane >= l0) & (lane < l0 + SUB)
            fwd[here] = jnp.where(pivots, jnp.where(lane - l0 == row, 1.0, 0.0), fwd[here])
            both = list(fwd)
            inv_d = jnp.zeros((SUB, LANES), jnp.float32)
            for i in range(0, SUB, 2):
                j = i + 1
                a, b, c = splat(cols[i], sub=i), splat(cols[i], sub=j), splat(cols[j], sub=j)
                inv_det, inv_a = 1.0 / (a * c - b * b), 1.0 / a
                pair = (row == i) | (row == j)
                ci = jnp.where(row == i, -1.0, jnp.where(row == j, 0.0, cols[i]))
                cj = jnp.where(row == j, -1.0, jnp.where(row == i, 0.0, cols[j]))
                mi = (ci * c - cj * b) * inv_det
                mj = (cj * a - ci * b) * inv_det
                fi = jnp.where(row > j, mi, jnp.where(row == j, b * inv_a, 0.0))
                fj = jnp.where(row > j, mj, 0.0)
                inv_d = jnp.where(row == i, inv_a, jnp.where(row == j, a * inv_det, inv_d))

                def eliminated(x):
                    x_i, x_j = splat(x, sub=i), splat(x, sub=j)
                    return jnp.where(pair, 0.0, x) - (mi * x_i + mj * x_j)

                for k in range(j + 1, SUB):
                    cols[k] = eliminated(cols[k])
                fwd = [x - (fi * splat(x, sub=i) + fj * splat(x, sub=j)) for x in fwd]
                if not last:
                    ahead = [eliminated(x) for x in ahead]
                    both = [eliminated(x) for x in both]
            if not last:
                cols = [
                    next_cols[k] - sum8([next_coef[m] * splat(ahead[k], sub=m) for m in range(SUB)])
                    for k in range(SUB)
                ]
                rows = [[splat(x, sub=k) for x in both] for k in range(SUB)]
                for g0 in range(r0 + SUB, p1, SUB):
                    old = [s[tile(g0, h)] for h in range(halves)]
                    coef = next_coef
                    if g0 > r0 + SUB:
                        coef = [splat(old[here], lane=l0 + k) for k in range(SUB)]
                    old[here] = jnp.where(pivots, 0.0, old[here])
                    for h in range(halves):
                        change = sum8([coef[k] * rows[k][h] for k in range(SUB)])
                        s[tile(g0, h)] = old[h] - change
            scale = jnp.sqrt(inv_d)
            for h in range(halves):
                s[tile(r0, h)] = fwd[h] * scale
        if p1 < order:
            panel = s[p0:p1, :]
            r = lax.broadcasted_iota(jnp.int32, panel.shape, 0)
            c = lax.broadcasted_iota(jnp.int32, panel.shape, 1)
            panel = jnp.where((c < p1) & (c > p0 + r), 0.0, panel)
            update = lax.dot_general(
                panel[:, p1:],
                panel,
                (((0,), (0,)), ((), ())),
                precision=lax.Precision.HIGHEST,
                preferred_element_type=jnp.float32,
            )
            c = lax.broadcasted_iota(jnp.int32, update.shape, 1)
            s[p1:, :] = jnp.where((c >= p0) & (c < p1), 0.0, s[p1:, :]) - update


def factor_kernel(core, mine, other, inv_t, s):
    first = core[0] == 0
    a, b = mine[...], other[...]
    unpack(s, jnp.concatenate([jnp.where(first, a, b), jnp.where(first, b, a)], axis=0))
    factor_in_place(s, s.shape[0])
    r = lax.broadcasted_iota(jnp.int32, s.shape, 0)
    c = lax.broadcasted_iota(jnp.int32, s.shape, 1)
    inv_t[...] = jnp.where(c <= r, s[...], 0.0)


def factor(core, mine, other):
    order = 2 * LANES
    vmem = pl.BlockSpec(memory_space=pltpu.VMEM)
    return pl.pallas_call(
        factor_kernel,
        out_shape=jax.ShapeDtypeStruct((order, order), jnp.float32),
        in_specs=[pl.BlockSpec(memory_space=pltpu.SMEM), vmem, vmem],
        out_specs=vmem,
        scratch_shapes=[pltpu.VMEM((order, order), jnp.float32)],
        compiler_params=pltpu.CompilerParams(vmem_limit_bytes=16 * 2**20),
        cost_estimate=pl.CostEstimate(flops=0, bytes_accessed=20 * 2**20, transcendentals=0),
    )(core, mine, other)


def basis_kernel(sketch, inv_t, basis, out, sems):
    inv = inv_t[...]
    hi = inv.astype(jnp.bfloat16)
    mid = (inv - hi.astype(jnp.float32)).astype(jnp.bfloat16)
    copies = []
    for n in range(sketch.shape[0] // CHUNK):
        rows = slice(n * CHUNK, (n + 1) * CHUNK)
        x = sketch[rows, :]
        total = None
        for part in (mid, hi):
            term = lax.dot_general(
                x, part, (((1,), (1,)), ((), ())), preferred_element_type=jnp.float32
            )
            total = term if total is None else total + term
        out[rows, :] = total
        copies.append(pltpu.make_async_copy(out.at[rows, :], basis.at[rows, :], sems.at[n]))
        copies[-1].start()
    for copy in copies:
        copy.wait()


def basis_of(sketch, inv_t):
    rows, order = sketch.shape
    vmem = pl.BlockSpec(memory_space=pltpu.VMEM)
    return pl.pallas_call(
        basis_kernel,
        out_shape=jax.ShapeDtypeStruct((rows, order), jnp.float32),
        in_specs=[vmem, vmem],
        out_specs=pl.BlockSpec(memory_space=pl.ANY),
        scratch_shapes=[
            pltpu.VMEM((rows, order), jnp.float32),
            pltpu.SemaphoreType.DMA((rows // CHUNK,)),
        ],
        compiler_params=pltpu.CompilerParams(vmem_limit_bytes=16 * 2**20),
        cost_estimate=pl.CostEstimate(
            flops=4 * rows * order * order, bytes_accessed=6 * rows * order, transcendentals=0
        ),
    )(sketch, inv_t)


def pack(gram):
    left, right = gram[:, :LANES], gram[:, LANES:]
    corners = jnp.where(
        lax.broadcasted_iota(jnp.int32, (PANEL, LANES), 1) < PANEL,
        pltpu.roll(right[3 * PANEL :], PANEL, 1),
        left[PANEL : 2 * PANEL],
    )
    return jnp.concatenate([left[:PANEL], corners, right[: 3 * PANEL]], axis=0)


def unpack(s, packed):
    corners = packed[PANEL : 2 * PANEL]
    s[:PANEL, :LANES] = packed[:PANEL]
    s[PANEL : 2 * PANEL, :LANES] = corners
    s[: 3 * PANEL, LANES:] = packed[2 * PANEL :]
    s[3 * PANEL :, LANES:] = pltpu.roll(corners, PANEL, 1)
    s[2 * PANEL :, :LANES] = jnp.zeros_like(corners, shape=(2 * PANEL, LANES))


def front_kernel(core, e, t, sketch, mine, theirs, kept, given, e_kept, t_kept, sems, *, scale):
    steps = e.shape[0] // LOAD
    load_t = pltpu.make_async_copy(t, t_kept, sems.at[steps])
    load_t.start()
    blocks = [slice(n * LOAD, (n + 1) * LOAD) for n in range(steps)]
    loads = [
        pltpu.make_async_copy(e.at[rows, :], e_kept.at[rows, :], sems.at[n])
        for n, rows in enumerate(blocks)
    ]
    for load in loads[:AHEAD]:
        load.start()
    load_t.wait()
    for n, rows in enumerate(blocks):
        loads[n].wait()
        if n + AHEAD < steps:
            loads[n + AHEAD].start()
        sketch[rows, :] = jnp.dot(
            e_kept[rows, :], t_kept[...], preferred_element_type=jnp.float32
        ).astype(jnp.bfloat16)
    s = sketch[...]
    by_rows = (((0,), (0,)), ((), ()))
    gram = lax.dot_general(s, s, by_rows, preferred_element_type=jnp.float32)
    packed = pack(gram * scale)
    half = packed.shape[0] // 2
    first = core[0] == 0
    mine[...] = jnp.where(first, packed[:half], packed[half:])
    theirs[...] = jnp.where(first, packed[half:], packed[:half])
    n_x, n_z, owned, order = kept.shape
    per_z = 2 * n_x * owned
    for z in range(0, n_z, 2):
        feats = slice(z * per_z, (z + 2) * per_z)
        c = lax.dot_general(
            e_kept[:, feats], s, by_rows, preferred_element_type=jnp.float32
        )
        c = c.reshape(2, n_x, 2, owned, order)
        for dz in range(2):
            for x in range(n_x):
                kept[x, z + dz] = jnp.where(first, c[dz, x, 0], c[dz, x, 1])
                given[x, z + dz] = jnp.where(first, c[dz, x, 1], c[dz, x, 0])


def front(core, e, t, rows_total, n_x, n_z):
    rows, feats = e.shape
    order = t.shape[1]
    gram_half = jax.ShapeDtypeStruct((5 * PANEL // 2, LANES), jnp.float32)
    owned = feats // (2 * n_x * n_z)
    cross_half = jax.ShapeDtypeStruct((n_x, n_z, owned, order), jnp.float32)
    vmem = pl.BlockSpec(memory_space=pltpu.VMEM)
    hbm = pl.BlockSpec(memory_space=pltpu.HBM)
    return pl.pallas_call(
        functools.partial(front_kernel, scale=1.0 / rows_total),
        out_shape=(
            jax.ShapeDtypeStruct((rows, order), jnp.bfloat16),
            gram_half,
            gram_half,
            cross_half,
            cross_half,
        ),
        in_specs=[pl.BlockSpec(memory_space=pltpu.SMEM), hbm, hbm],
        out_specs=(vmem,) * 5,
        scratch_shapes=[
            pltpu.VMEM(e.shape, e.dtype),
            pltpu.VMEM(t.shape, t.dtype),
            pltpu.SemaphoreType.DMA((rows // LOAD + 1,)),
        ],
        compiler_params=pltpu.CompilerParams(vmem_limit_bytes=52 * 2**20),
    )(core, e, t)


def pick(x, index):
    return lax.dynamic_index_in_dim(x, index, 0, keepdims=False)


def body(embeddings, test_matrix):
    n_wide = lax.axis_size("wide")
    rows_total = embeddings.shape[0] * n_wide * lax.axis_size("narrow")
    place = lax.axis_index("wide")
    core, x_at, z_at = place & 1, place >> 1 & 3, place >> 3
    at = core.reshape(1)
    sketch, mine, theirs, kept, given = front(at, embeddings, test_matrix, rows_total, 4, 8)
    groups_x = [[z * 8 + x * 2 + c for x in range(4)] for z in range(8) for c in range(2)]
    groups_z = [[z * 8 + r for z in range(8)] for r in range(8)]
    mine = mine + shifted(theirs, "wide", other_core)
    mine, given = barrier(mine, given)
    kept = kept + shifted(given, "wide", other_core)
    kept = lax.all_to_all(kept, "wide", 0, 0, tiled=True, axis_index_groups=groups_x)
    mine = mine + shifted(mine, "wide", Z_PAIR)
    mine, = barrier(mine)
    mine = sum4([mine] + [shifted(mine, "wide", t) for t in (Z_NEXT, Z_TWO, Z_THREE)])
    kept = jnp.sum(kept, axis=0)
    kept = lax.all_to_all(kept, "wide", 0, 0, tiled=True, axis_index_groups=groups_z)
    mine, = barrier(mine)
    mine = over_four(mine, "narrow", flip)
    mine, = barrier(mine)
    mine = over_four(mine, "wide", along_x)
    mine, = barrier(mine)
    other = shifted(mine, "wide", other_core)
    inv_t = factor(at, mine, other)
    inv_t, kept = barrier(inv_t, kept)
    kept = jnp.sum(kept, axis=0)
    kept = over_four(kept, "narrow", flip)
    basis_rows = basis_of(sketch, inv_t)
    loadings = (
        lax.dot_general(
            kept, inv_t, (((1,), (1,)), ((), ())), precision=lax.Precision.HIGHEST
        )
        / rows_total
    )
    return (basis_rows, loadings)


CROSS = "a2a"


def solution(mesh):
    in_specs = (P(("wide", "narrow"), None), P())
    out_specs = (P(("wide", "narrow"), None), P("wide", None))
    return jax.shard_map(body, mesh=mesh, in_specs=in_specs, out_specs=out_specs, check_vma=False)
```

```python
import functools

import jax
import jax.numpy as jnp
from jax import lax
from jax.experimental import pallas as pl
from jax.experimental.pallas import tpu as pltpu
from jax.sharding import PartitionSpec as P

LANES = 128
SUB = 8
PANEL = 64
CHUNK = 256
LOAD = 512
AHEAD = 2


def barrier(*values):
    return lax.optimization_barrier(values)


def shifted(x, axis, target):
    return lax.ppermute(x, axis, [(i, target(i)) for i in range(lax.axis_size(axis))])


def along_z(target):
    return lambda i: (target(i >> 3) % 8) << 3 | i & 7


Z_PAIR = along_z(lambda z: z ^ 1)
Z_NEXT = along_z(lambda z: z + 1 if z % 2 else z - 1)
Z_TWO = along_z(lambda z: z + 2 if z % 2 else z - 2)
Z_THREE = along_z(lambda z: z + 3 if z % 2 else z - 3)


def along_x(bits):
    return lambda i: i ^ bits << 1


def other_core(i):
    return i ^ 1


def flip(bits):
    return lambda i: i ^ bits


def sum4(parts):
    return (parts[0] + parts[1]) + (parts[2] + parts[3])


def over_four(x, axis, flipped):
    one, three, two = (shifted(x, axis, flipped(k)) for k in (1, 3, 2))
    return sum4([x, one, two, three])


def splat(x, sub=None, lane=None):
    if lane is not None:
        x = x[:, lane : lane + 1]
    if sub is not None:
        x = x[sub : sub + 1, :]
    return jnp.broadcast_to(x, (SUB, LANES))


def sum8(parts):
    return sum4(parts[:4]) + sum4(parts[4:])


def factor_in_place(s, order):
    halves = order // LANES
    row = lax.broadcasted_iota(jnp.int32, (SUB, LANES), 0)
    lane = lax.broadcasted_iota(jnp.int32, (SUB, LANES), 1)

    def tile(r, h):
        return (slice(r, r + SUB), slice(LANES * h, LANES * (h + 1)))

    for p0 in range(0, order, PANEL):
        p1, here = p0 + PANEL, p0 // LANES
        cols = [splat(s[tile(p0, here)], lane=p0 % LANES + k) for k in range(SUB)]
        for r0 in range(p0, p1, SUB):
            l0 = r0 % LANES
            last = r0 + SUB >= p1
            fwd = [s[tile(r0, h)] for h in range(halves)]
            if not last:
                ahead = [splat(fwd[here], lane=l0 + SUB + k) for k in range(SUB)]
                below = s[tile(r0 + SUB, here)]
                next_coef = [splat(below, lane=l0 + k) for k in range(SUB)]
                next_cols = [splat(below, lane=l0 + SUB + k) for k in range(SUB)]
            pivots = (lane >= l0) & (lane < l0 + SUB)
            fwd[here] = jnp.where(pivots, jnp.where(lane - l0 == row, 1.0, 0.0), fwd[here])
            both = list(fwd)
            inv_d = jnp.zeros((SUB, LANES), jnp.float32)
            for i in range(0, SUB, 2):
                j = i + 1
                a, b, c = splat(cols[i], sub=i), splat(cols[i], sub=j), splat(cols[j], sub=j)
                inv_a = 1.0 / a
                ratio = b * inv_a
                inv_c = 1.0 / (c - b * ratio)
                pair = (row == i) | (row == j)
                ci = jnp.where(row == i, -1.0, jnp.where(row == j, 0.0, cols[i]))
                cj = jnp.where(row == j, -1.0, jnp.where(row == i, 0.0, cols[j]))
                mj = (cj - ci * ratio) * inv_c
                mi = ci * inv_a - mj * ratio
                fi = jnp.where(row > j, mi, jnp.where(row == j, ratio, 0.0))
                fj = jnp.where(row > j, mj, 0.0)
                inv_d = jnp.where(row == i, inv_a, jnp.where(row == j, inv_c, inv_d))

                def eliminated(x):
                    x_i, x_j = splat(x, sub=i), splat(x, sub=j)
                    return jnp.where(pair, 0.0, x) - (mi * x_i + mj * x_j)

                for k in range(j + 1, SUB):
                    cols[k] = eliminated(cols[k])
                fwd = [x - (fi * splat(x, sub=i) + fj * splat(x, sub=j)) for x in fwd]
                if not last:
                    ahead = [eliminated(x) for x in ahead]
                    both = [eliminated(x) for x in both]
            if not last:
                cols = [
                    next_cols[k] - sum8([next_coef[m] * splat(ahead[k], sub=m) for m in range(SUB)])
                    for k in range(SUB)
                ]
                rows = [[splat(x, sub=k) for x in both] for k in range(SUB)]
                for g0 in range(r0 + SUB, p1, SUB):
                    old = [s[tile(g0, h)] for h in range(halves)]
                    coef = next_coef
                    if g0 > r0 + SUB:
                        coef = [splat(old[here], lane=l0 + k) for k in range(SUB)]
                    old[here] = jnp.where(pivots, 0.0, old[here])
                    for h in range(halves):
                        change = sum8([coef[k] * rows[k][h] for k in range(SUB)])
                        s[tile(g0, h)] = old[h] - change
            scale = jnp.sqrt(inv_d)
            for h in range(halves):
                s[tile(r0, h)] = fwd[h] * scale
        if p1 < order:
            panel = s[p0:p1, :]
            r = lax.broadcasted_iota(jnp.int32, panel.shape, 0)
            c = lax.broadcasted_iota(jnp.int32, panel.shape, 1)
            panel = jnp.where((c < p1) & (c > p0 + r), 0.0, panel)
            update = lax.dot_general(
                panel[:, p1:],
                panel,
                (((0,), (0,)), ((), ())),
                precision=lax.Precision.HIGHEST,
                preferred_element_type=jnp.float32,
            )
            c = lax.broadcasted_iota(jnp.int32, update.shape, 1)
            s[p1:, :] = jnp.where((c >= p0) & (c < p1), 0.0, s[p1:, :]) - update


def factor_kernel(core, mine, other, inv_t, s):
    first = core[0] == 0
    a, b = mine[...], other[...]
    unpack(s, jnp.concatenate([jnp.where(first, a, b), jnp.where(first, b, a)], axis=0))
    factor_in_place(s, s.shape[0])
    r = lax.broadcasted_iota(jnp.int32, s.shape, 0)
    c = lax.broadcasted_iota(jnp.int32, s.shape, 1)
    inv_t[...] = jnp.where(c <= r, s[...], 0.0)


def factor(core, mine, other):
    order = 2 * LANES
    vmem = pl.BlockSpec(memory_space=pltpu.VMEM)
    return pl.pallas_call(
        factor_kernel,
        out_shape=jax.ShapeDtypeStruct((order, order), jnp.float32),
        in_specs=[pl.BlockSpec(memory_space=pltpu.SMEM), vmem, vmem],
        out_specs=vmem,
        scratch_shapes=[pltpu.VMEM((order, order), jnp.float32)],
        compiler_params=pltpu.CompilerParams(vmem_limit_bytes=16 * 2**20),
        cost_estimate=pl.CostEstimate(flops=0, bytes_accessed=20 * 2**20, transcendentals=0),
    )(core, mine, other)


def basis_kernel(sketch, inv_t, basis, out, sems):
    inv = inv_t[...]
    hi = inv.astype(jnp.bfloat16)
    mid = (inv - hi.astype(jnp.float32)).astype(jnp.bfloat16)
    copies = []
    for n in range(sketch.shape[0] // CHUNK):
        rows = slice(n * CHUNK, (n + 1) * CHUNK)
        x = sketch[rows, :]
        total = None
        for part in (mid, hi):
            term = lax.dot_general(
                x, part, (((1,), (1,)), ((), ())), preferred_element_type=jnp.float32
            )
            total = term if total is None else total + term
        out[rows, :] = total
        copies.append(pltpu.make_async_copy(out.at[rows, :], basis.at[rows, :], sems.at[n]))
        copies[-1].start()
    for copy in copies:
        copy.wait()


def basis_of(sketch, inv_t):
    rows, order = sketch.shape
    vmem = pl.BlockSpec(memory_space=pltpu.VMEM)
    return pl.pallas_call(
        basis_kernel,
        out_shape=jax.ShapeDtypeStruct((rows, order), jnp.float32),
        in_specs=[vmem, vmem],
        out_specs=pl.BlockSpec(memory_space=pl.ANY),
        scratch_shapes=[
            pltpu.VMEM((rows, order), jnp.float32),
            pltpu.SemaphoreType.DMA((rows // CHUNK,)),
        ],
        compiler_params=pltpu.CompilerParams(vmem_limit_bytes=16 * 2**20),
        cost_estimate=pl.CostEstimate(
            flops=4 * rows * order * order, bytes_accessed=6 * rows * order, transcendentals=0
        ),
    )(sketch, inv_t)


def pack(gram):
    left, right = gram[:, :LANES], gram[:, LANES:]
    corners = jnp.where(
        lax.broadcasted_iota(jnp.int32, (PANEL, LANES), 1) < PANEL,
        pltpu.roll(right[3 * PANEL :], PANEL, 1),
        left[PANEL : 2 * PANEL],
    )
    return jnp.concatenate([left[:PANEL], corners, right[: 3 * PANEL]], axis=0)


def unpack(s, packed):
    corners = packed[PANEL : 2 * PANEL]
    s[:PANEL, :LANES] = packed[:PANEL]
    s[PANEL : 2 * PANEL, :LANES] = corners
    s[: 3 * PANEL, LANES:] = packed[2 * PANEL :]
    s[3 * PANEL :, LANES:] = pltpu.roll(corners, PANEL, 1)
    s[2 * PANEL :, :LANES] = jnp.zeros_like(corners, shape=(2 * PANEL, LANES))


def front_kernel(core, e, t, sketch, mine, theirs, kept, given, e_kept, t_kept, sems, *, scale):
    steps = e.shape[0] // LOAD
    load_t = pltpu.make_async_copy(t, t_kept, sems.at[steps])
    load_t.start()
    blocks = [slice(n * LOAD, (n + 1) * LOAD) for n in range(steps)]
    loads = [
        pltpu.make_async_copy(e.at[rows, :], e_kept.at[rows, :], sems.at[n])
        for n, rows in enumerate(blocks)
    ]
    for load in loads[:AHEAD]:
        load.start()
    load_t.wait()
    for n, rows in enumerate(blocks):
        loads[n].wait()
        if n + AHEAD < steps:
            loads[n + AHEAD].start()
        sketch[rows, :] = jnp.dot(
            e_kept[rows, :], t_kept[...], preferred_element_type=jnp.float32
        ).astype(jnp.bfloat16)
    s = sketch[...]
    by_rows = (((0,), (0,)), ((), ()))
    gram = lax.dot_general(s, s, by_rows, preferred_element_type=jnp.float32)
    packed = pack(gram * scale)
    half = packed.shape[0] // 2
    first = core[0] == 0
    mine[...] = jnp.where(first, packed[:half], packed[half:])
    theirs[...] = jnp.where(first, packed[half:], packed[:half])
    n_x, n_z, owned, order = kept.shape
    per_z = 2 * n_x * owned
    for z in range(0, n_z, 2):
        feats = slice(z * per_z, (z + 2) * per_z)
        c = lax.dot_general(
            e_kept[:, feats], s, by_rows, preferred_element_type=jnp.float32
        )
        c = c.reshape(2, n_x, 2, owned, order)
        for dz in range(2):
            for x in range(n_x):
                kept[x, z + dz] = jnp.where(first, c[dz, x, 0], c[dz, x, 1])
                given[x, z + dz] = jnp.where(first, c[dz, x, 1], c[dz, x, 0])


def front(core, e, t, rows_total, n_x, n_z):
    rows, feats = e.shape
    order = t.shape[1]
    gram_half = jax.ShapeDtypeStruct((5 * PANEL // 2, LANES), jnp.float32)
    owned = feats // (2 * n_x * n_z)
    cross_half = jax.ShapeDtypeStruct((n_x, n_z, owned, order), jnp.float32)
    vmem = pl.BlockSpec(memory_space=pltpu.VMEM)
    hbm = pl.BlockSpec(memory_space=pltpu.HBM)
    return pl.pallas_call(
        functools.partial(front_kernel, scale=1.0 / rows_total),
        out_shape=(
            jax.ShapeDtypeStruct((rows, order), jnp.bfloat16),
            gram_half,
            gram_half,
            cross_half,
            cross_half,
        ),
        in_specs=[pl.BlockSpec(memory_space=pltpu.SMEM), hbm, hbm],
        out_specs=(vmem,) * 5,
        scratch_shapes=[
            pltpu.VMEM(e.shape, e.dtype),
            pltpu.VMEM(t.shape, t.dtype),
            pltpu.SemaphoreType.DMA((rows // LOAD + 1,)),
        ],
        compiler_params=pltpu.CompilerParams(vmem_limit_bytes=52 * 2**20),
    )(core, e, t)


def body(embeddings, test_matrix):
    n_wide = lax.axis_size("wide")
    rows_total = embeddings.shape[0] * n_wide * lax.axis_size("narrow")
    place = lax.axis_index("wide")
    at = (place & 1).reshape(1)
    sketch, mine, theirs, kept, given = front(at, embeddings, test_matrix, rows_total, 4, 8)
    groups_x = [[z * 8 + x * 2 + c for x in range(4)] for z in range(8) for c in range(2)]
    groups_z = [[z * 8 + r for z in range(8)] for r in range(8)]
    mine = mine + shifted(theirs, "wide", other_core)
    mine, given = barrier(mine, given)
    kept = kept + shifted(given, "wide", other_core)
    kept = lax.all_to_all(kept, "wide", 0, 0, tiled=True, axis_index_groups=groups_x)
    mine = mine + shifted(mine, "wide", Z_PAIR)
    mine, = barrier(mine)
    mine = sum4([mine] + [shifted(mine, "wide", t) for t in (Z_NEXT, Z_TWO, Z_THREE)])
    kept = jnp.sum(kept, axis=0)
    kept = lax.all_to_all(kept, "wide", 0, 0, tiled=True, axis_index_groups=groups_z)
    mine, = barrier(mine)
    mine = over_four(mine, "narrow", flip)
    mine, = barrier(mine)
    mine = over_four(mine, "wide", along_x)
    mine, = barrier(mine)
    other = shifted(mine, "wide", other_core)
    inv_t = factor(at, mine, other)
    inv_t, kept = barrier(inv_t, kept)
    kept = jnp.sum(kept, axis=0)
    kept = over_four(kept, "narrow", flip)
    basis_rows = basis_of(sketch, inv_t)
    loadings = (
        lax.dot_general(
            kept, inv_t, (((1,), (1,)), ((), ())), precision=lax.Precision.HIGHEST
        )
        / rows_total
    )
    return (basis_rows, loadings)


def solution(mesh):
    in_specs = (P(("wide", "narrow"), None), P())
    out_specs = (P(("wide", "narrow"), None), P("wide", None))
    return jax.shard_map(body, mesh=mesh, in_specs=in_specs, out_specs=out_specs, check_vma=False)
```

```python
import functools

import jax
import jax.numpy as jnp
from jax import lax
from jax.experimental import pallas as pl
from jax.experimental.pallas import tpu as pltpu
from jax.sharding import PartitionSpec as P

LANES = 128
SUB = 8
PANEL = 64
CHUNK = 256
LOAD = 512
AHEAD = 2


def barrier(*values):
    return lax.optimization_barrier(values)


def shifted(x, axis, target):
    return lax.ppermute(x, axis, [(i, target(i)) for i in range(lax.axis_size(axis))])


def along_z(target):
    return lambda i: (target(i >> 3) % 8) << 3 | i & 7


Z_PAIR = along_z(lambda z: z ^ 1)
Z_NEXT = along_z(lambda z: z + 1 if z % 2 else z - 1)
Z_TWO = along_z(lambda z: z + 2 if z % 2 else z - 2)
Z_THREE = along_z(lambda z: z + 3 if z % 2 else z - 3)


def along_x(bits):
    return lambda i: i ^ bits << 1


def other_core(i):
    return i ^ 1


def flip(bits):
    return lambda i: i ^ bits


def sum4(parts):
    return (parts[0] + parts[1]) + (parts[2] + parts[3])


def over_four(x, axis, flipped):
    one, three, two = (shifted(x, axis, flipped(k)) for k in (1, 3, 2))
    return sum4([x, one, two, three])


def splat(x, sub=None, lane=None):
    if lane is not None:
        x = x[:, lane : lane + 1]
    if sub is not None:
        x = x[sub : sub + 1, :]
    return jnp.broadcast_to(x, (SUB, LANES))


def sum8(parts):
    return sum4(parts[:4]) + sum4(parts[4:])


def factor_in_place(s, order):
    halves = order // LANES
    row = lax.broadcasted_iota(jnp.int32, (SUB, LANES), 0)
    lane = lax.broadcasted_iota(jnp.int32, (SUB, LANES), 1)

    def tile(r, h):
        return (slice(r, r + SUB), slice(LANES * h, LANES * (h + 1)))

    for p0 in range(0, order, PANEL):
        p1, here = p0 + PANEL, p0 // LANES
        cols = [splat(s[tile(p0, here)], lane=p0 % LANES + k) for k in range(SUB)]
        for r0 in range(p0, p1, SUB):
            l0 = r0 % LANES
            last = r0 + SUB >= p1
            fwd = [s[tile(r0, h)] for h in range(halves)]
            if not last:
                ahead = [splat(fwd[here], lane=l0 + SUB + k) for k in range(SUB)]
                below = s[tile(r0 + SUB, here)]
                next_coef = [splat(below, lane=l0 + k) for k in range(SUB)]
                next_cols = [splat(below, lane=l0 + SUB + k) for k in range(SUB)]
            pivots = (lane >= l0) & (lane < l0 + SUB)
            fwd[here] = jnp.where(pivots, jnp.where(lane - l0 == row, 1.0, 0.0), fwd[here])
            both = list(fwd)
            inv_d = jnp.zeros((SUB, LANES), jnp.float32)
            for i in range(0, SUB, 2):
                j = i + 1
                a, b, c = splat(cols[i], sub=i), splat(cols[i], sub=j), splat(cols[j], sub=j)
                inv_a = 1.0 / a
                ratio = b * inv_a
                inv_c = 1.0 / (c - b * ratio)
                pair = (row == i) | (row == j)
                ci = jnp.where(row == i, -1.0, jnp.where(row == j, 0.0, cols[i]))
                cj = jnp.where(row == j, -1.0, jnp.where(row == i, 0.0, cols[j]))
                mj = (cj - ci * ratio) * inv_c
                mi = ci * inv_a - mj * ratio
                fi = jnp.where(row > j, mi, jnp.where(row == j, ratio, 0.0))
                fj = jnp.where(row > j, mj, 0.0)
                inv_d = jnp.where(row == i, inv_a, jnp.where(row == j, inv_c, inv_d))

                def eliminated(x):
                    x_i, x_j = splat(x, sub=i), splat(x, sub=j)
                    return jnp.where(pair, 0.0, x) - (mi * x_i + mj * x_j)

                for k in range(j + 1, SUB):
                    cols[k] = eliminated(cols[k])
                fwd = [x - (fi * splat(x, sub=i) + fj * splat(x, sub=j)) for x in fwd]
                if not last:
                    ahead = [eliminated(x) for x in ahead]
                    both = [eliminated(x) for x in both]
            if not last:
                cols = [
                    next_cols[k] - sum8([next_coef[m] * splat(ahead[k], sub=m) for m in range(SUB)])
                    for k in range(SUB)
                ]
                rows = [[splat(x, sub=k) for x in both] for k in range(SUB)]
                for g0 in range(r0 + SUB, p1, SUB):
                    old = [s[tile(g0, h)] for h in range(halves)]
                    coef = next_coef
                    if g0 > r0 + SUB:
                        coef = [splat(old[here], lane=l0 + k) for k in range(SUB)]
                    old[here] = jnp.where(pivots, 0.0, old[here])
                    for h in range(halves):
                        change = sum8([coef[k] * rows[k][h] for k in range(SUB)])
                        s[tile(g0, h)] = old[h] - change
            scale = jnp.sqrt(inv_d)
            for h in range(halves):
                s[tile(r0, h)] = fwd[h] * scale
        if p1 < order:
            panel = s[p0:p1, :]
            r = lax.broadcasted_iota(jnp.int32, panel.shape, 0)
            c = lax.broadcasted_iota(jnp.int32, panel.shape, 1)
            panel = jnp.where((c < p1) & (c > p0 + r), 0.0, panel)
            update = lax.dot_general(
                panel[:, p1:],
                panel,
                (((0,), (0,)), ((), ())),
                precision=lax.Precision.HIGHEST,
                preferred_element_type=jnp.float32,
            )
            c = lax.broadcasted_iota(jnp.int32, update.shape, 1)
            s[p1:, :] = jnp.where((c >= p0) & (c < p1), 0.0, s[p1:, :]) - update


def factor_kernel(core, mine, other, inv_t, s):
    first = core[0] == 0
    a, b = mine[...], other[...]
    unpack(s, jnp.concatenate([jnp.where(first, a, b), jnp.where(first, b, a)], axis=0))
    factor_in_place(s, s.shape[0])
    r = lax.broadcasted_iota(jnp.int32, s.shape, 0)
    c = lax.broadcasted_iota(jnp.int32, s.shape, 1)
    inv_t[...] = jnp.where(c <= r, s[...], 0.0)


def factor(core, mine, other):
    order = 2 * LANES
    vmem = pl.BlockSpec(memory_space=pltpu.VMEM)
    return pl.pallas_call(
        factor_kernel,
        out_shape=jax.ShapeDtypeStruct((order, order), jnp.float32),
        in_specs=[pl.BlockSpec(memory_space=pltpu.SMEM), vmem, vmem],
        out_specs=vmem,
        scratch_shapes=[pltpu.VMEM((order, order), jnp.float32)],
        compiler_params=pltpu.CompilerParams(vmem_limit_bytes=16 * 2**20),
        cost_estimate=pl.CostEstimate(flops=0, bytes_accessed=20 * 2**20, transcendentals=0),
    )(core, mine, other)


def basis_kernel(sketch, inv_t, basis, out, sems):
    inv = inv_t[...]
    hi = inv.astype(jnp.bfloat16)
    mid = (inv - hi.astype(jnp.float32)).astype(jnp.bfloat16)
    copies = []
    for n in range(sketch.shape[0] // CHUNK):
        rows = slice(n * CHUNK, (n + 1) * CHUNK)
        x = sketch[rows, :]
        total = None
        for part in (mid, hi):
            term = lax.dot_general(
                x, part, (((1,), (1,)), ((), ())), preferred_element_type=jnp.float32
            )
            total = term if total is None else total + term
        out[rows, :] = total
        copies.append(pltpu.make_async_copy(out.at[rows, :], basis.at[rows, :], sems.at[n]))
        copies[-1].start()
    for copy in copies:
        copy.wait()


def basis_of(sketch, inv_t):
    rows, order = sketch.shape
    vmem = pl.BlockSpec(memory_space=pltpu.VMEM)
    return pl.pallas_call(
        basis_kernel,
        out_shape=jax.ShapeDtypeStruct((rows, order), jnp.float32),
        in_specs=[vmem, vmem],
        out_specs=pl.BlockSpec(memory_space=pl.ANY),
        scratch_shapes=[
            pltpu.VMEM((rows, order), jnp.float32),
            pltpu.SemaphoreType.DMA((rows // CHUNK,)),
        ],
        compiler_params=pltpu.CompilerParams(vmem_limit_bytes=16 * 2**20),
        cost_estimate=pl.CostEstimate(
            flops=4 * rows * order * order, bytes_accessed=6 * rows * order, transcendentals=0
        ),
    )(sketch, inv_t)


def pack(gram):
    left, right = gram[:, :LANES], gram[:, LANES:]
    corners = jnp.where(
        lax.broadcasted_iota(jnp.int32, (PANEL, LANES), 1) < PANEL,
        pltpu.roll(right[3 * PANEL :], PANEL, 1),
        left[PANEL : 2 * PANEL],
    )
    return jnp.concatenate([left[:PANEL], corners, right[: 3 * PANEL]], axis=0)


def unpack(s, packed):
    corners = packed[PANEL : 2 * PANEL]
    s[:PANEL, :LANES] = packed[:PANEL]
    s[PANEL : 2 * PANEL, :LANES] = corners
    s[: 3 * PANEL, LANES:] = packed[2 * PANEL :]
    s[3 * PANEL :, LANES:] = pltpu.roll(corners, PANEL, 1)
    s[2 * PANEL :, :LANES] = jnp.zeros_like(corners, shape=(2 * PANEL, LANES))


def front_kernel(
    core, e, t, sketch_out, mine, theirs, kept, given, e_kept, t_kept, sketch, sems, *, scale
):
    steps = e.shape[0] // LOAD
    load_t = pltpu.make_async_copy(t, t_kept, sems.at[steps])
    load_t.start()
    blocks = [slice(n * LOAD, (n + 1) * LOAD) for n in range(steps)]
    loads = [
        pltpu.make_async_copy(e.at[rows, :], e_kept.at[rows, :], sems.at[n])
        for n, rows in enumerate(blocks)
    ]
    for load in loads[:AHEAD]:
        load.start()
    load_t.wait()
    for n, rows in enumerate(blocks):
        loads[n].wait()
        if n + AHEAD < steps:
            loads[n + AHEAD].start()
        sketch[rows, :] = jnp.dot(
            e_kept[rows, :], t_kept[...], preferred_element_type=jnp.float32
        ).astype(jnp.bfloat16)
    store = pltpu.make_async_copy(sketch, sketch_out, sems.at[steps + 1])
    store.start()
    s = sketch[...]
    by_rows = (((0,), (0,)), ((), ()))
    gram = lax.dot_general(s, s, by_rows, preferred_element_type=jnp.float32)
    packed = pack(gram * scale)
    half = packed.shape[0] // 2
    first = core[0] == 0
    mine[...] = jnp.where(first, packed[:half], packed[half:])
    theirs[...] = jnp.where(first, packed[half:], packed[:half])
    n_x, n_z, owned, order = kept.shape
    per_z = 2 * n_x * owned
    for z in range(0, n_z, 2):
        feats = slice(z * per_z, (z + 2) * per_z)
        c = lax.dot_general(
            e_kept[:, feats], s, by_rows, preferred_element_type=jnp.float32
        )
        c = c.reshape(2, n_x, 2, owned, order)
        for dz in range(2):
            for x in range(n_x):
                kept[x, z + dz] = jnp.where(first, c[dz, x, 0], c[dz, x, 1])
                given[x, z + dz] = jnp.where(first, c[dz, x, 1], c[dz, x, 0])
    store.wait()


def front(core, e, t, rows_total, n_x, n_z):
    rows, feats = e.shape
    order = t.shape[1]
    gram_half = jax.ShapeDtypeStruct((5 * PANEL // 2, LANES), jnp.float32)
    owned = feats // (2 * n_x * n_z)
    cross_half = jax.ShapeDtypeStruct((n_x, n_z, owned, order), jnp.float32)
    vmem = pl.BlockSpec(memory_space=pltpu.VMEM)
    hbm = pl.BlockSpec(memory_space=pltpu.HBM)
    return pl.pallas_call(
        functools.partial(front_kernel, scale=1.0 / rows_total),
        out_shape=(
            jax.ShapeDtypeStruct((rows, order), jnp.bfloat16),
            gram_half,
            gram_half,
            cross_half,
            cross_half,
        ),
        in_specs=[pl.BlockSpec(memory_space=pltpu.SMEM), hbm, hbm],
        out_specs=(pl.BlockSpec(memory_space=pl.ANY),) + (vmem,) * 4,
        scratch_shapes=[
            pltpu.VMEM(e.shape, e.dtype),
            pltpu.VMEM(t.shape, t.dtype),
            pltpu.VMEM((rows, order), e.dtype),
            pltpu.SemaphoreType.DMA((rows // LOAD + 2,)),
        ],
        compiler_params=pltpu.CompilerParams(vmem_limit_bytes=52 * 2**20),
    )(core, e, t)


def body(embeddings, test_matrix):
    n_wide = lax.axis_size("wide")
    rows_total = embeddings.shape[0] * n_wide * lax.axis_size("narrow")
    place = lax.axis_index("wide")
    at = (place & 1).reshape(1)
    sketch, mine, theirs, kept, given = front(at, embeddings, test_matrix, rows_total, 4, 8)
    groups_x = [[z * 8 + x * 2 + c for x in range(4)] for z in range(8) for c in range(2)]
    groups_z = [[z * 8 + r for z in range(8)] for r in range(8)]
    mine = mine + shifted(theirs, "wide", other_core)
    mine, given = barrier(mine, given)
    kept = kept + shifted(given, "wide", other_core)
    kept = lax.all_to_all(kept, "wide", 0, 0, tiled=True, axis_index_groups=groups_x)
    mine = mine + shifted(mine, "wide", Z_PAIR)
    mine, = barrier(mine)
    mine = sum4([mine] + [shifted(mine, "wide", t) for t in (Z_NEXT, Z_TWO, Z_THREE)])
    kept = jnp.sum(kept, axis=0)
    kept = lax.all_to_all(kept, "wide", 0, 0, tiled=True, axis_index_groups=groups_z)
    mine, = barrier(mine)
    mine = over_four(mine, "narrow", flip)
    mine, = barrier(mine)
    mine = over_four(mine, "wide", along_x)
    mine, = barrier(mine)
    other = shifted(mine, "wide", other_core)
    inv_t = factor(at, mine, other)
    inv_t, kept = barrier(inv_t, kept)
    kept = jnp.sum(kept, axis=0)
    kept = over_four(kept, "narrow", flip)
    basis_rows = basis_of(sketch, inv_t)
    loadings = (
        lax.dot_general(
            kept, inv_t, (((1,), (1,)), ((), ())), precision=lax.Precision.HIGHEST
        )
        / rows_total
    )
    return (basis_rows, loadings)


def solution(mesh):
    in_specs = (P(("wide", "narrow"), None), P())
    out_specs = (P(("wide", "narrow"), None), P("wide", None))
    return jax.shard_map(body, mesh=mesh, in_specs=in_specs, out_specs=out_specs, check_vma=False)
```
